32 devices in a mesh: users: 4 (over y, x), items: 8 (over z, core).
Axes of the slice: x: 2, y: 2, z: 4, core: 2. Of those that a mesh axis runs over, the one named last changes fastest.
Arguments:
- user_emb: float32 [32768, 256], P(('users', 'items')), may hold values from -0.375 to 0.375
- item_emb: float32 [2048, 256], P('items'), may hold values from -0.375 to 0.375
- pos_blocks: int32 [32, 4], P(('users', 'items')), may hold values from 0 to 7, all different within a row
- neg_blocks: int32 [2], replicated, may hold values from 0 to 15
Outputs:
- user_new: float32 [32768, 256], P(('users', 'items'))
- item_new: float32 [2048, 256], P('items')
The draws below stay inside these ranges and needn't reach their ends.
Inputs may be any that keep to these rules, and one draw needn't show every extreme that they name: `pos_blocks`: each row lists 4 different item blocks, and every item block is listed by some user block. `neg_blocks`: ids may repeat.
All inputs are finite; a program needn't handle non-finite values.
Results may differ from the reference program's by a relative error of at most 0.0003.
Values sent between devices are 32-bit elements; how exact they have to be, the bound alone decides.
A program may use at most 64 MiB of HBM per device.

```python
import math
import jax
import jax.numpy as jnp
import numpy as np
from jax import lax

E = 256
UROWS = 1024
IROWS = 256
NEGROWS = 128
NPOS = 4
NNEG = 2
NSUB = 2
BLOCKS = 32
USERS = 32768
ITEMS = 2048
N_USERS = 4
N_ITEMS = 8


def cluster_axes(key):
    base = jax.random.normal(jax.random.fold_in(key, 101), (16, E), jnp.float32)
    return jnp.clip(base, -3.0, 3.0) / math.sqrt(E)


def clustered_rows(key, shared, noise, low, high):
    count = noise.shape[0]
    width = shared.shape[1]
    first = jax.random.randint(jax.random.fold_in(key, 1), (count,), 0, 16)
    second = (first + jax.random.randint(jax.random.fold_in(key, 2), (count,), 1, 16)) % 16
    sign_first = (2 * jax.random.randint(jax.random.fold_in(key, 3), (count,), 0, 2) - 1).astype(jnp.float32)
    sign_second = (2 * jax.random.randint(jax.random.fold_in(key, 4), (count,), 0, 2) - 1).astype(jnp.float32)
    amp_first = jax.random.uniform(jax.random.fold_in(key, 5), (count,), jnp.float32, low, high)
    amp_second = jax.random.uniform(jax.random.fold_in(key, 6), (count,), jnp.float32, 0.3, 0.55)
    rows = (sign_first * amp_first)[:, None] * jnp.take(shared, first, axis=0)
    rows = rows + (sign_second * amp_second)[:, None] * jnp.take(shared, second, axis=0)
    rows = rows + noise / math.sqrt(width)
    return jnp.clip(rows, -0.375, 0.375)


def draw_user_emb(key, part):
    shared = cluster_axes(key)
    key = jax.random.fold_in(key, 3)
    noise_key = jax.random.fold_in(key, 11)
    noise = jnp.clip(jax.random.normal(noise_key, (USERS, E), jnp.float32), -3.0, 3.0) * 0.3
    return clustered_rows(key, shared, noise, 0.55, 0.85)


def draw_item_emb(key, part):
    shared = cluster_axes(key)
    key = jax.random.fold_in(key, 5)
    noise_key = jax.random.fold_in(key, 13)
    noise = jnp.clip(jax.random.normal(noise_key, (ITEMS, E), jnp.float32), -3.0, 3.0) * 0.3
    return clustered_rows(key, shared, noise, 0.55, 0.85)


def rank_table(amount, lean):
    portions = [(1 << 20) // math.isqrt(grade ** lean) + 1 for grade in range(1, amount + 1)]
    spread = 1 + sum(portions) // (1 << 30)
    return np.cumsum(np.array([max(1, weight // spread) for weight in portions]))


def ranked_ids(key, extent, count, slope):
    grid = rank_table(count, slope)
    ticket = jax.random.randint(jax.random.fold_in(key, 1), extent, 0, int(grid[count - 1]))
    grade = jnp.searchsorted(jnp.asarray(grid, jnp.int32), ticket, side="right")
    return jax.random.permutation(jax.random.fold_in(key, 2), count)[grade].astype(jnp.int32)


def distinct(key, rows, amount, top, lift):
    ranking = jax.random.permutation(jax.random.fold_in(key, 1), amount)
    pull = ranking
    for power in range(3):
        pull = pull * pull // amount
    pull = pull * lift // amount
    chance = jax.random.randint(jax.random.fold_in(key, 2), (rows, amount), 0, 4096) + pull
    fixed_rows = jax.random.permutation(jax.random.fold_in(key, 3), rows)[jnp.arange(amount) % rows]
    chance = jnp.where(jnp.arange(rows)[:, None] == fixed_rows[None, :], 1 << 14, chance)
    score = chance * amount + jnp.arange(amount)
    return lax.top_k(score.astype(jnp.int32), top)[1].astype(jnp.int32)


def setup_inputs(seed: int = 0) -> dict:
    splits = jax.random.split(jax.random.key(seed), 5)
    user_emb = draw_user_emb(jax.random.fold_in(splits[4], 71), 0)
    item_emb = draw_item_emb(jax.random.fold_in(splits[4], 71), 0)
    pos_blocks = distinct(splits[2], BLOCKS, N_ITEMS, NPOS, 8192)
    neg_blocks = ranked_ids(splits[3], (NNEG,), N_ITEMS * NSUB, 2)
    return dict(user_emb=user_emb, item_emb=item_emb, pos_blocks=pos_blocks, neg_blocks=neg_blocks)


SHARPNESS = 8.0
MARGIN = 2.0

def distances(left, right):
    products = jnp.dot(left, right.T, precision=lax.Precision.HIGHEST, preferred_element_type=jnp.float32)
    return lax.optimization_barrier(jnp.sum(left * left, axis=1))[:, None] + lax.optimization_barrier(jnp.sum(right * right, axis=1))[None, :] - 2.0 * products

def positive_weights(squared):
    return jax.nn.sigmoid(SHARPNESS * (squared - MARGIN))

def negative_weights(squared):
    return -jax.nn.sigmoid(SHARPNESS * (MARGIN - squared))

def pair_terms(weights, left, right):
    left_term = 2.0 * (lax.optimization_barrier(jnp.sum(weights, axis=1))[:, None] * left - jnp.dot(weights, right, precision=lax.Precision.HIGHEST, preferred_element_type=jnp.float32))
    right_term = 2.0 * (lax.optimization_barrier(jnp.sum(weights, axis=0))[:, None] * right - jnp.dot(weights.T, left, precision=lax.Precision.HIGHEST, preferred_element_type=jnp.float32))
    return (left_term, right_term)

def clipped(field):
    norms = jnp.sqrt(lax.optimization_barrier(jnp.sum(field * field, axis=1, keepdims=True)))
    return field / jnp.maximum(norms, 1.0)

def reference(user_emb, item_emb, pos_blocks, neg_blocks):
    block_count = USERS // UROWS
    negatives = jnp.concatenate([lax.dynamic_slice_in_dim(item_emb, (neg_blocks[k] * NEGROWS).astype(jnp.int32), NEGROWS, 0) for k in range(NNEG)], axis=0)
    user_blocks = user_emb.reshape(block_count, UROWS, E)

    def per_block(carry, scan_inputs):
        item_grad, neg_grad = carry
        user_block, pair_list = scan_inputs
        user_grad = jnp.zeros((UROWS, E), jnp.float32)
        for k in range(NPOS):
            offset = (pair_list[k] * IROWS).astype(jnp.int32)
            item_block = lax.dynamic_slice_in_dim(item_emb, offset, IROWS, 0)
            weights = positive_weights(distances(user_block, item_block))
            left_term, right_term = pair_terms(weights, user_block, item_block)
            user_grad = user_grad + left_term
            current = lax.dynamic_slice_in_dim(item_grad, offset, IROWS, 0)
            item_grad = lax.dynamic_update_slice_in_dim(item_grad, current + right_term, offset, 0)
        weights = negative_weights(distances(user_block, negatives))
        left_term, right_term = pair_terms(weights, user_block, negatives)
        return ((item_grad, neg_grad + right_term), user_grad + left_term)
    start_carry = (jnp.zeros((ITEMS, E), jnp.float32), jnp.zeros((NNEG * NEGROWS, E), jnp.float32))
    (item_grad, neg_grad), user_grads = lax.scan(per_block, start_carry, (user_blocks, pos_blocks))
    for k in range(NNEG):
        offset = (neg_blocks[k] * NEGROWS).astype(jnp.int32)
        current = lax.dynamic_slice_in_dim(item_grad, offset, NEGROWS, 0)
        item_grad = lax.dynamic_update_slice_in_dim(item_grad, current + neg_grad[k * NEGROWS:(k + 1) * NEGROWS], offset, 0)
    user_rate = 0.5 / (NPOS * IROWS + NNEG * NEGROWS)
    item_rate = 0.5 / (NPOS * UROWS * N_USERS)
    user_new = clipped(user_emb - user_rate * user_grads.reshape(USERS, E))
    item_new = clipped(item_emb - item_rate * item_grad)
    return (user_new, item_new)
```

```python
import functools

import jax
import jax.numpy as jnp
from jax import lax
from jax.experimental import pallas as pl
from jax.experimental.pallas import tpu as pltpu
from jax.sharding import PartitionSpec as P

NEGROWS = 128
SHARPNESS = 8.0
MARGIN = 2.0
CHUNK = 512
MESH = pl.DeviceIdType.MESH


def split(x):
    high = x.astype(jnp.bfloat16)
    return high, (x - high.astype(jnp.float32)).astype(jnp.bfloat16)


def dot(a, b):
    return jnp.dot(a, b, preferred_element_type=jnp.float32)


def dot3(ah, al, bh, bl):
    return dot(ah, bh) + (dot(ah, bl) + dot(al, bh))


def clipped(field):
    norms = jnp.sqrt(jnp.sum(field * field, axis=1, keepdims=True))
    return field / jnp.maximum(norms, 1.0)


def kernel(
    n_users, n_items, user_rate, item_rate,
    user_ref, item_ref, pos_ref, neg_ref,
    user_out, item_out,
    mate, flags, uh, ul, uth, utl, ac, vbuf, vt, vth, vtl, vh, vl, bc,
    term, r1, psum, r2, gt, gu, rs, gsend, gmate,
    mate_s, mate_r, flag_s, flag_r, gm_s, gm_r,
    g1_s, g1_r, g2_s, g2_r, r1_s, r1_r, r2_s, r2_r, r3_s, r3_r,
):
    u = lax.axis_index("users")
    i = lax.axis_index("items")
    depth = n_items // 2
    z = i // 2
    c = i % 2
    other = 2 * z + (1 - c)
    rows, width = user_ref.shape
    cols = item_ref.shape[0]
    neg_count = neg_ref.shape[0]
    pair_count = pos_ref.shape[1]
    vrows = cols // n_users
    trows = width // n_users
    chunks = rows // CHUNK

    def plane(d):
        return ((u + d) % n_users, i)

    def up(s):
        return (u, 2 * ((z + s) % depth) + c)

    def down(s):
        return (u, 2 * ((z + depth - s) % depth) + c)

    def remote(src, dst, send, recv, where):
        return pltpu.make_async_remote_copy(
            src_ref=src, dst_ref=dst, send_sem=send, recv_sem=recv, device_id=where, device_id_type=MESH
        )

    barrier = pltpu.get_barrier_semaphore()
    pl.semaphore_signal(barrier, inc=1, device_id=(u, other), device_id_type=MESH)
    for d in range(1, n_users):
        pl.semaphore_signal(barrier, inc=1, device_id=plane(d), device_id_type=MESH)
    for s in range(1, depth):
        pl.semaphore_signal(barrier, inc=1, device_id=up(s), device_id_type=MESH)

    lane = lax.broadcasted_iota(jnp.int32, (8, 128), 1)
    listed = jnp.zeros((8, 128), jnp.float32)
    for k in range(pair_count):
        listed = listed + jnp.where(lane == pos_ref[0, k], 1.0, 0.0)
    flags[0] = listed

    pl.semaphore_wait(barrier, 1 + (n_users - 1) + (depth - 1))

    own_v = pl.ds(pl.multiple_of(u * vrows, vrows), vrows)
    own_t = pl.ds(pl.multiple_of(u * trows, trows), trows)

    g1 = {}
    for s in range(1, depth):
        g1[s] = remote(item_ref.at[own_v], vbuf.at[s, own_v], g1_s.at[s], g1_r.at[s], down(s))
        g1[s].start()
    mate_copy = remote(user_ref, mate, mate_s, mate_r, (u, other))
    mate_copy.start()
    flag_copy = remote(flags.at[0], flags.at[1], flag_s, flag_r, (u, other))
    flag_copy.start()

    def prepare_users(h, ref):
        @pl.loop(0, chunks)
        def _(k):
            at = pl.ds(pl.multiple_of(k * CHUNK, CHUNK), CHUNK)
            x = ref[at]
            ac[h, at] = 4.0 * jnp.sum(x * x, axis=1, keepdims=True) - 8.0
            high, low = split(-8.0 * x)
            uh[h, at] = high
            ul[h, at] = low
            high, low = split(x.T)
            uth[h, k] = high
            utl[h, k] = low
            gu[h, at] = jnp.zeros((CHUNK, width), jnp.float32)
            rs[h, at] = jnp.zeros((CHUNK, 128), jnp.float32)

    def prepare_items(s):
        x = item_ref[...] if s == 0 else vbuf[s]
        turned = x.T
        vt[s] = turned
        vth[s], vtl[s] = split(turned)
        vh[s], vl[s] = split(x)
        bc[s] = jnp.broadcast_to(4.0 * jnp.sum(turned * turned, axis=0, keepdims=True), (8, cols))
        term[s] = jnp.zeros((width, cols), jnp.float32)

    def unit(s, h):
        block = 2 * ((z + s) % depth) + c
        listed = jnp.sum(jnp.where(lane == block, flags[h], 0.0), axis=1, keepdims=True)[0:1]
        sub = block * (cols // NEGROWS) + lax.broadcasted_iota(jnp.int32, (1, cols), 1) // NEGROWS
        repeats = jnp.zeros((1, cols), jnp.float32)
        for k in range(neg_count):
            repeats = repeats + jnp.where(sub == neg_ref[k], 1.0, 0.0)
        slope = 0.5 * (listed + repeats)
        level = slope - repeats
        ahead = bc[s, 0:1]

        def step(k, total):
            at = pl.ds(pl.multiple_of(k * CHUNK, CHUNK), CHUNK)
            t = dot3(uh[h, at], ul[h, at], vth[s], vtl[s]) + (ac[h, at] + ahead)
            w = slope * jnp.tanh(t) + level
            wh, wl = split(w)
            gu[h, at] += dot3(wh, wl, vh[s], vl[s])
            part = w[:, 0:128]
            for b in range(1, cols // 128):
                part = part + w[:, b * 128 : (b + 1) * 128]
            rs[h, at] += part
            term[s] -= dot3(uth[h, k], utl[h, k], wh, wl)
            return total + jnp.sum(w, axis=0, keepdims=True)

        total = lax.fori_loop(0, chunks, step, jnp.zeros((1, cols), jnp.float32))
        term[s] += total * vt[s]

    g2 = {}

    def forward(s):
        g1[s].wait_recv()
        for d in range(1, n_users):
            g2[s, d] = remote(
                vbuf.at[s, own_v], vbuf.at[s, own_v], g2_s.at[s, d], g2_r.at[s, d], plane(d)
            )
            g2[s, d].start()

    r1c = {}
    r2c = {}

    def scatter(s):
        for d in range(1, n_users):
            to = (u + d) % n_users
            piece = pl.ds(pl.multiple_of(to * trows, trows), trows)
            r1c[s, d] = remote(
                term.at[s, piece], r1.at[d, s], r1_s.at[s, d], r1_r.at[s, d], plane(d)
            )
            r1c[s, d].start()

    def gather_sum(s):
        x = term[s, own_t]
        for d in range(1, n_users):
            r1c[s, d].wait_recv()
            x = x + r1[d, s]
        psum[s] = x
        if s:
            r2c[s] = remote(psum.at[s], r2.at[s], r2_s.at[s], r2_r.at[s], up(s))
            r2c[s].start()

    prepare_users(0, user_ref)
    prepare_items(0)
    forward(1)
    unit(0, 0)
    for s in range(2, depth):
        forward(s)
    mate_copy.wait_recv()
    flag_copy.wait_recv()
    prepare_users(1, mate)
    for s in range(1, depth):
        for d in range(1, n_users):
            g2[s, d].wait_recv()
        prepare_items(s)
        unit(s, 0)
        unit(s, 1)
        scatter(s)
        if s > 1:
            gather_sum(s - 1)
    unit(0, 1)
    scatter(0)
    gather_sum(depth - 1)

    def grad(h, ref, at):
        return jnp.sum(rs[h, at], axis=1, keepdims=True) * ref[at] - gu[h, at]

    @pl.loop(0, chunks)
    def _(k):
        at = pl.ds(pl.multiple_of(k * CHUNK, CHUNK), CHUNK)
        gsend[at] = grad(1, mate, at)

    gm_copy = remote(gsend, gmate, gm_s, gm_r, (u, other))
    gm_copy.start()

    gather_sum(0)
    x = psum[0]
    for s in range(1, depth):
        r2c[s].wait_recv()
        x = x + r2[s]
    gt[own_t] = x
    r3c = {}
    for d in range(1, n_users):
        r3c[d] = remote(gt.at[own_t], gt.at[own_t], r3_s.at[d], r3_r.at[d], plane(d))
        r3c[d].start()

    gm_copy.wait_recv()

    @pl.loop(0, chunks)
    def _(k):
        at = pl.ds(pl.multiple_of(k * CHUNK, CHUNK), CHUNK)
        total = grad(0, user_ref, at) + gmate[at]
        user_out[at] = clipped(user_ref[at] - (2.0 * user_rate) * total)

    for d in range(1, n_users):
        r3c[d].wait_recv()
    item_out[...] = clipped(item_ref[...] - (2.0 * item_rate) * gt[...].T)

    mate_copy.wait_send()
    flag_copy.wait_send()
    gm_copy.wait_send()
    for s in range(1, depth):
        g1[s].wait_send()
        r2c[s].wait_send()
        for d in range(1, n_users):
            g2[s, d].wait_send()
    for d in range(1, n_users):
        for s in range(depth):
            r1c[s, d].wait_send()
        r3c[d].wait_send()


def on_device(n_users, n_items, user_emb, item_emb, pos_blocks, neg_blocks):
    rows, width = user_emb.shape
    cols = item_emb.shape[0]
    neg_count = neg_blocks.shape[0]
    pair_count = pos_blocks.shape[1]
    depth = n_items // 2
    chunks = rows // CHUNK
    user_rate = 0.5 / (pair_count * cols + neg_count * NEGROWS)
    item_rate = 0.5 / (pair_count * rows * n_users)
    trows = width // n_users
    f32, b16 = jnp.float32, jnp.bfloat16
    dma = pltpu.SemaphoreType.DMA
    vmem = pl.BlockSpec(memory_space=pltpu.VMEM)
    smem = pl.BlockSpec(memory_space=pltpu.SMEM)
    scratch = [
        pltpu.VMEM((rows, width), f32),
        pltpu.VMEM((2, 8, 128), f32),
        pltpu.VMEM((2, rows, width), b16),
        pltpu.VMEM((2, rows, width), b16),
        pltpu.VMEM((2, chunks, width, CHUNK), b16),
        pltpu.VMEM((2, chunks, width, CHUNK), b16),
        pltpu.VMEM((2, rows, 1), f32),
        pltpu.VMEM((depth, cols, width), f32),
        pltpu.VMEM((depth, width, cols), f32),
        pltpu.VMEM((depth, width, cols), b16),
        pltpu.VMEM((depth, width, cols), b16),
        pltpu.VMEM((depth, cols, width), b16),
        pltpu.VMEM((depth, cols, width), b16),
        pltpu.VMEM((depth, 8, cols), f32),
        pltpu.VMEM((depth, width, cols), f32),
        pltpu.VMEM((n_users, depth, trows, cols), f32),
        pltpu.VMEM((depth, trows, cols), f32),
        pltpu.VMEM((depth, trows, cols), f32),
        pltpu.VMEM((width, cols), f32),
        pltpu.VMEM((2, rows, width), f32),
        pltpu.VMEM((2, rows, 128), f32),
        pltpu.VMEM((rows, width), f32),
        pltpu.VMEM((rows, width), f32),
        dma, dma, dma, dma, dma, dma,
        dma((depth,)), dma((depth,)),
        dma((depth, n_users)), dma((depth, n_users)),
        dma((depth, n_users)), dma((depth, n_users)),
        dma((depth,)), dma((depth,)),
        dma((n_users,)), dma((n_users,)),
    ]
    return pl.pallas_call(
        functools.partial(kernel, n_users, n_items, user_rate, item_rate),
        out_shape=(
            jax.ShapeDtypeStruct((rows, width), f32),
            jax.ShapeDtypeStruct((cols, width), f32),
        ),
        in_specs=[vmem, vmem, smem, smem],
        out_specs=(vmem, vmem),
        scratch_shapes=scratch,
        compiler_params=pltpu.CompilerParams(
            collective_id=0, has_side_effects=True, vmem_limit_bytes=48 * 1024 * 1024
        ),
        name="metric_step",
    )(user_emb, item_emb, pos_blocks, neg_blocks)


def solution(mesh):
    return jax.shard_map(
        functools.partial(on_device, mesh.shape["users"], mesh.shape["items"]),
        mesh=mesh,
        in_specs=(P(("users", "items"), None), P("items", None), P(("users", "items"), None), P()),
        out_specs=(P(("users", "items"), None), P("items", None)),
        check_vma=False,
    )
```

```python
import functools

import jax
import jax.numpy as jnp
from jax import lax
from jax.experimental import pallas as pl
from jax.experimental.pallas import tpu as pltpu
from jax.sharding import PartitionSpec as P

NEGROWS = 128
SHARPNESS = 8.0
MARGIN = 2.0
CHUNK = 1024
MESH = pl.DeviceIdType.MESH


def split(x):
    high = x.astype(jnp.bfloat16)
    return high, (x - high.astype(jnp.float32)).astype(jnp.bfloat16)


def dot(a, b):
    return jnp.dot(a, b, preferred_element_type=jnp.float32)


def dot3(ah, al, bh, bl):
    return dot(ah, bh) + (dot(ah, bl) + dot(al, bh))


def clipped(field):
    norms = jnp.sqrt(jnp.sum(field * field, axis=1, keepdims=True))
    return field / jnp.maximum(norms, 1.0)


def kernel(
    n_users, n_items, user_rate, item_rate,
    user_hbm, item_hbm, pos_hbm, neg_hbm,
    user_out, item_out,
    user_ref, item_ref, pos_ref, neg_ref, load_s,
    mate, flags, uh, ul, uth, utl, ac, vbuf, vt, vth, vtl, vh, vl, bc,
    term, r1, psum, r2, gt, gu, rs, gsend, gmate,
    mate_s, mate_r, flag_s, flag_r, gm_s, gm_r,
    g1_s, g1_r, g2_s, g2_r, r1_s, r1_r, r2_s, r2_r, r3_s, r3_r,
):
    u = lax.axis_index("users")
    i = lax.axis_index("items")
    depth = n_items // 2
    z = i // 2
    c = i % 2
    other = 2 * z + (1 - c)
    rows, width = user_ref.shape
    cols = item_ref.shape[0]
    neg_count = neg_ref.shape[0]
    pair_count = pos_ref.shape[1]
    vrows = cols // n_users
    trows = width // n_users
    chunks = rows // CHUNK

    loads = [
        pltpu.make_async_copy(src, dst, load_s.at[n])
        for n, (src, dst) in enumerate(
            [(pos_hbm, pos_ref), (neg_hbm, neg_ref), (item_hbm, item_ref), (user_hbm, user_ref)]
        )
    ]
    for load in loads:
        load.start()

    def plane(d):
        return ((u + d) % n_users, i)

    def up(s):
        return (u, 2 * ((z + s) % depth) + c)

    def down(s):
        return (u, 2 * ((z + depth - s) % depth) + c)

    def remote(src, dst, send, recv, where):
        return pltpu.make_async_remote_copy(
            src_ref=src, dst_ref=dst, send_sem=send, recv_sem=recv, device_id=where, device_id_type=MESH
        )

    barrier = pltpu.get_barrier_semaphore()
    pl.semaphore_signal(barrier, inc=1, device_id=(u, other), device_id_type=MESH)
    for d in range(1, n_users):
        pl.semaphore_signal(barrier, inc=1, device_id=plane(d), device_id_type=MESH)
    for s in range(1, depth):
        pl.semaphore_signal(barrier, inc=1, device_id=up(s), device_id_type=MESH)

    loads[0].wait()
    loads[1].wait()
    lane = lax.broadcasted_iota(jnp.int32, (8, 128), 1)
    listed = jnp.zeros((8, 128), jnp.float32)
    for k in range(pair_count):
        listed = listed + jnp.where(lane == pos_ref[0, k], 1.0, 0.0)
    flags[0] = listed

    pl.semaphore_wait(barrier, 1 + (n_users - 1) + (depth - 1))

    own_v = pl.ds(pl.multiple_of(u * vrows, vrows), vrows)
    own_t = pl.ds(pl.multiple_of(u * trows, trows), trows)

    g1 = {}
    for s in range(1, depth):
        g1[s] = remote(item_hbm.at[own_v], vbuf.at[s, own_v], g1_s.at[s], g1_r.at[s], down(s))
        g1[s].start()
    mate_copy = remote(user_hbm, mate, mate_s, mate_r, (u, other))
    mate_copy.start()
    flag_copy = remote(flags.at[0], flags.at[1], flag_s, flag_r, (u, other))
    flag_copy.start()

    def prepare_users(h, ref):
        @pl.loop(0, chunks)
        def _(k):
            at = pl.ds(pl.multiple_of(k * CHUNK, CHUNK), CHUNK)
            x = ref[at]
            ac[h, at] = 4.0 * jnp.sum(x * x, axis=1, keepdims=True) - 8.0
            high, low = split(-8.0 * x)
            uh[h, at] = high
            ul[h, at] = low
            high, low = split(x.T)
            uth[h, k] = high
            utl[h, k] = low
            gu[h, at] = jnp.zeros((CHUNK, width), jnp.float32)
            rs[h, at] = jnp.zeros((CHUNK, 128), jnp.float32)

    def prepare_items(s):
        x = item_ref[...] if s == 0 else vbuf[s]
        turned = x.T
        vt[s] = turned
        vth[s], vtl[s] = split(turned)
        vh[s], vl[s] = split(x)
        bc[s] = jnp.broadcast_to(4.0 * jnp.sum(turned * turned, axis=0, keepdims=True), (8, cols))
        term[s] = jnp.zeros((width, cols), jnp.float32)

    def unit(s, h):
        block = 2 * ((z + s) % depth) + c
        listed = jnp.sum(jnp.where(lane == block, flags[h], 0.0), axis=1, keepdims=True)[0:1]
        sub = block * (cols // NEGROWS) + lax.broadcasted_iota(jnp.int32, (1, cols), 1) // NEGROWS
        repeats = jnp.zeros((1, cols), jnp.float32)
        for k in range(neg_count):
            repeats = repeats + jnp.where(sub == neg_ref[k], 1.0, 0.0)
        slope = 0.5 * (listed + repeats)
        level = slope - repeats
        ahead = bc[s, 0:1]

        def step(k, total):
            at = pl.ds(pl.multiple_of(k * CHUNK, CHUNK), CHUNK)
            t = dot3(uh[h, at], ul[h, at], vth[s], vtl[s]) + (ac[h, at] + ahead)
            w = slope * jnp.tanh(t) + level
            wh, wl = split(w)
            gu[h, at] += dot3(wh, wl, vh[s], vl[s])
            part = w[:, 0:128]
            for b in range(1, cols // 128):
                part = part + w[:, b * 128 : (b + 1) * 128]
            rs[h, at] += part
            term[s] -= dot3(uth[h, k], utl[h, k], wh, wl)
            return total + jnp.sum(w, axis=0, keepdims=True)

        total = lax.fori_loop(0, chunks, step, jnp.zeros((1, cols), jnp.float32))
        term[s] += total * vt[s]

    g2 = {}

    def forward(s):
        g1[s].wait_recv()
        for d in range(1, n_users):
            g2[s, d] = remote(
                vbuf.at[s, own_v], vbuf.at[s, own_v], g2_s.at[s, d], g2_r.at[s, d], plane(d)
            )
            g2[s, d].start()

    r1c = {}
    r2c = {}

    def scatter(s):
        for d in range(1, n_users):
            to = (u + d) % n_users
            piece = pl.ds(pl.multiple_of(to * trows, trows), trows)
            r1c[s, d] = remote(
                term.at[s, piece], r1.at[d, s], r1_s.at[s, d], r1_r.at[s, d], plane(d)
            )
            r1c[s, d].start()

    def gather_sum(s):
        x = term[s, own_t]
        for d in range(1, n_users):
            r1c[s, d].wait_recv()
            x = x + r1[d, s]
        psum[s] = x
        if s:
            r2c[s] = remote(psum.at[s], r2.at[s], r2_s.at[s], r2_r.at[s], up(s))
            r2c[s].start()

    loads[3].wait()
    prepare_users(0, user_ref)
    loads[2].wait()
    prepare_items(0)
    forward(1)
    unit(0, 0)
    for s in range(2, depth):
        forward(s)
    mate_copy.wait_recv()
    flag_copy.wait_recv()
    prepare_users(1, mate)
    for s in range(1, depth):
        for d in range(1, n_users):
            g2[s, d].wait_recv()
        prepare_items(s)
        unit(s, 0)
        unit(s, 1)
        scatter(s)
        if s > 1:
            gather_sum(s - 1)
    unit(0, 1)
    scatter(0)
    def grad(h, ref, at):
        return jnp.sum(rs[h, at], axis=1, keepdims=True) * ref[at] - gu[h, at]

    @pl.loop(0, chunks)
    def _(k):
        at = pl.ds(pl.multiple_of(k * CHUNK, CHUNK), CHUNK)
        gsend[at] = grad(1, mate, at)

    gm_copy = remote(gsend, gmate, gm_s, gm_r, (u, other))
    gm_copy.start()
    gather_sum(depth - 1)
    gather_sum(0)

    @pl.loop(0, chunks)
    def _(k):
        at = pl.ds(pl.multiple_of(k * CHUNK, CHUNK), CHUNK)
        gu[0, at] = user_ref[at] - (2.0 * user_rate) * grad(0, user_ref, at)

    x = psum[0]
    for s in range(1, depth):
        r2c[s].wait_recv()
        x = x + r2[s]
    gt[own_t] = x
    r3c = {}
    for d in range(1, n_users):
        r3c[d] = remote(gt.at[own_t], gt.at[own_t], r3_s.at[d], r3_r.at[d], plane(d))
        r3c[d].start()

    gm_copy.wait_recv()

    @pl.loop(0, chunks)
    def _(k):
        at = pl.ds(pl.multiple_of(k * CHUNK, CHUNK), CHUNK)
        user_out[at] = clipped(gu[0, at] - (2.0 * user_rate) * gmate[at])

    for d in range(1, n_users):
        r3c[d].wait_recv()
    item_out[...] = clipped(item_ref[...] - (2.0 * item_rate) * gt[...].T)

    mate_copy.wait_send()
    flag_copy.wait_send()
    gm_copy.wait_send()
    for s in range(1, depth):
        g1[s].wait_send()
        r2c[s].wait_send()
        for d in range(1, n_users):
            g2[s, d].wait_send()
    for d in range(1, n_users):
        for s in range(depth):
            r1c[s, d].wait_send()
        r3c[d].wait_send()


def on_device(n_users, n_items, user_emb, item_emb, pos_blocks, neg_blocks):
    rows, width = user_emb.shape
    cols = item_emb.shape[0]
    neg_count = neg_blocks.shape[0]
    pair_count = pos_blocks.shape[1]
    depth = n_items // 2
    chunks = rows // CHUNK
    user_rate = 0.5 / (pair_count * cols + neg_count * NEGROWS)
    item_rate = 0.5 / (pair_count * rows * n_users)
    trows = width // n_users
    f32, b16 = jnp.float32, jnp.bfloat16
    dma = pltpu.SemaphoreType.DMA
    vmem = pl.BlockSpec(memory_space=pltpu.VMEM)
    hbm = pl.BlockSpec(memory_space=pltpu.HBM)
    scratch = [
        pltpu.VMEM((rows, width), f32),
        pltpu.VMEM((cols, width), f32),
        pltpu.SMEM(pos_blocks.shape, jnp.int32),
        pltpu.SMEM(neg_blocks.shape, jnp.int32),
        dma((4,)),
        pltpu.VMEM((rows, width), f32),
        pltpu.VMEM((2, 8, 128), f32),
        pltpu.VMEM((2, rows, width), b16),
        pltpu.VMEM((2, rows, width), b16),
        pltpu.VMEM((2, chunks, width, CHUNK), b16),
        pltpu.VMEM((2, chunks, width, CHUNK), b16),
        pltpu.VMEM((2, rows, 1), f32),
        pltpu.VMEM((depth, cols, width), f32),
        pltpu.VMEM((depth, width, cols), f32),
        pltpu.VMEM((depth, width, cols), b16),
        pltpu.VMEM((depth, width, cols), b16),
        pltpu.VMEM((depth, cols, width), b16),
        pltpu.VMEM((depth, cols, width), b16),
        pltpu.VMEM((depth, 8, cols), f32),
        pltpu.VMEM((depth, width, cols), f32),
        pltpu.VMEM((n_users, depth, trows, cols), f32),
        pltpu.VMEM((depth, trows, cols), f32),
        pltpu.VMEM((depth, trows, cols), f32),
        pltpu.VMEM((width, cols), f32),
        pltpu.VMEM((2, rows, width), f32),
        pltpu.VMEM((2, rows, 128), f32),
        pltpu.VMEM((rows, width), f32),
        pltpu.VMEM((rows, width), f32),
        dma, dma, dma, dma, dma, dma,
        dma((depth,)), dma((depth,)),
        dma((depth, n_users)), dma((depth, n_users)),
        dma((depth, n_users)), dma((depth, n_users)),
        dma((depth,)), dma((depth,)),
        dma((n_users,)), dma((n_users,)),
    ]
    return pl.pallas_call(
        functools.partial(kernel, n_users, n_items, user_rate, item_rate),
        out_shape=(
            jax.ShapeDtypeStruct((rows, width), f32),
            jax.ShapeDtypeStruct((cols, width), f32),
        ),
        in_specs=[pl.BlockSpec(memory_space=pl.ANY)] * 4,
        out_specs=(vmem, vmem),
        scratch_shapes=scratch,
        compiler_params=pltpu.CompilerParams(
            collective_id=0, has_side_effects=True, vmem_limit_bytes=60 * 1024 * 1024
        ),
        name="metric_step",
    )(user_emb, item_emb, pos_blocks, neg_blocks)


def solution(mesh):
    return jax.shard_map(
        functools.partial(on_device, mesh.shape["users"], mesh.shape["items"]),
        mesh=mesh,
        in_specs=(P(("users", "items"), None), P("items", None), P(("users", "items"), None), P()),
        out_specs=(P(("users", "items"), None), P("items", None)),
        check_vma=False,
    )
```
